128 devices in a mesh: row: 8 (over y, core), col: 16 (over z, x).
Axes of the slice: x: 4, y: 4, z: 4, core: 2. Of those that a mesh axis runs over, the one named last changes fastest.
Arguments:
- pattern: int32 [16, 32, 9], P('row', 'col'), may hold values from 0 to 1, as said below
- start: float32 [16, 32, 9, 128, 128], P('row', 'col'), may hold values from -1 to 1, as said below
Outputs:
- sign_estimate: float32 [16, 32, 9, 128, 128], P('row', 'col')
The draws below stay inside these ranges and needn't reach their ends.
Inputs may be any that keep to these rules, and one draw needn't show every extreme that they name: Offset 4 (the site itself) is always 1; the pattern is symmetric: pattern[p, k] = pattern[p + step(k), 8 - k], and 0 where the neighbour lies outside the grid; about 8 ones a site. Symmetric: start[p, k] is the transpose of start[p + step(k), 8 - k] wherever that neighbour lies in the grid.
All inputs are finite; a program needn't handle non-finite values.
Results may differ from the reference program's by a relative error of at most 0.0001.
Values sent between devices are 32-bit elements; how exact they have to be, the bound alone decides.
A program may use at most 320 MiB of HBM per device.

```python
import jax
import jax.numpy as jnp
from jax import lax

BLOCK = 128
ITERS = 2
GA = 16
GB = 32


def move_sites(array, step_row, step_col):
    widths = ((1, 1), (1, 1)) + ((0, 0),) * (array.ndim - 2)
    padded = jnp.pad(array, widths)
    return padded[1 - step_row:1 - step_row + GA, 1 - step_col:1 - step_col + GB]


def draw_pattern(key, part):
    key = jax.random.fold_in(key, 11)
    picks = jax.random.randint(key, (GA, GB, 4), 0, 8)
    forward = (picks < 7).astype(jnp.int32)
    inside = jnp.ones((GA, GB), jnp.int32)
    columns = []
    for offset in range(9):
        step_row = offset // 3 - 1
        step_col = offset % 3 - 1
        if offset == 4:
            columns.append(inside)
        elif offset > 4:
            columns.append(forward[:, :, offset - 5] * move_sites(inside, -step_row, -step_col))
        else:
            columns.append(move_sites(forward[:, :, 3 - offset], -step_row, -step_col))
    return jnp.stack(columns, axis=-1)


def draw_start(key, part):
    key = jax.random.fold_in(key, 23)
    noise_key, diag_key, sign_key, couple_key, couple_sign_key = jax.random.split(key, 5)
    shape = (GA, GB, 9, BLOCK, BLOCK)
    noise = jax.random.truncated_normal(noise_key, -4.0, 4.0, shape, jnp.float32) * 0.003
    magnitude = jax.random.uniform(diag_key, (GA, GB, BLOCK), jnp.float32, 0.3, 0.8)
    coupling = jax.random.uniform(couple_key, (GA, GB, 4), jnp.float32, 0.05, 0.09)
    signs = 2.0 * jax.random.randint(sign_key, (GA, GB, BLOCK), 0, 2).astype(jnp.float32) - 1.0
    couple_signs = 2.0 * jax.random.randint(couple_sign_key, (GA, GB, 4), 0, 2).astype(jnp.float32) - 1.0
    eye = jnp.eye(BLOCK, dtype=jnp.float32)
    center = 0.5 * (noise[:, :, 4] + jnp.swapaxes(noise[:, :, 4], -1, -2)) + (signs * magnitude)[:, :, :, None] * eye
    forward = []
    for slot in range(4):
        forward.append(noise[:, :, 5 + slot] + (couple_signs * coupling)[:, :, slot, None, None] * eye)
    blocks = []
    for offset in range(9):
        step_row = offset // 3 - 1
        step_col = offset % 3 - 1
        if offset == 4:
            blocks.append(center)
        elif offset > 4:
            blocks.append(forward[offset - 5])
        else:
            blocks.append(jnp.swapaxes(move_sites(forward[3 - offset], -step_row, -step_col), -1, -2))
    return jnp.stack(blocks, axis=2)


def setup_inputs(seed: int = 0) -> dict:
    key_list = jax.random.split(jax.random.key(seed), 3)
    return {
        "pattern": draw_pattern(jax.random.fold_in(key_list[2], 71), 0),
        "start": draw_start(jax.random.fold_in(key_list[2], 71), 0),
    }


def multiply(left, right_ext):
    row_count = left.shape[0]
    col_count = left.shape[1]
    results = []
    for offset in range(9):
        step_row = offset // 3 - 1
        step_col = offset % 3 - 1
        total = jnp.zeros((row_count, col_count) + left.shape[3:], jnp.float32)
        for inner in range(9):
            inner_row = inner // 3 - 1
            inner_col = inner % 3 - 1
            back_row = step_row - inner_row
            back_col = step_col - inner_col
            if back_row < -1 or back_row > 1 or back_col < -1 or back_col > 1:
                continue
            target = (back_row + 1) * 3 + back_col + 1
            piece = right_ext[1 + inner_row:1 + inner_row + row_count, 1 + inner_col:1 + inner_col + col_count, target]
            total = total + jnp.einsum("abij,abjk->abik", left[:, :, inner], piece, precision=lax.Precision.HIGHEST, preferred_element_type=jnp.float32)
        results.append(total)
    return jnp.stack(results, axis=2)


def reference(pattern, start):
    keep = pattern.astype(jnp.float32)[:, :, :, None, None]
    widths = ((1, 1), (1, 1), (0, 0), (0, 0), (0, 0))
    iterate = start * keep
    for sweep in range(ITERS):
        square = multiply(iterate, jnp.pad(iterate, widths)) * keep
        cube = multiply(iterate, jnp.pad(square, widths)) * keep
        iterate = 1.5 * iterate - 0.5 * cube
    return iterate
```

```python
import functools

import jax
import jax.numpy as jnp
from jax import lax
from jax.experimental import pallas as pl
from jax.experimental.pallas import tpu as pltpu
from jax.sharding import PartitionSpec as P

MESH = pl.DeviceIdType.MESH
SIDES = ((0, 1), (0, -1), (1, 0), (-1, 0))
INNER = (((0, 0), ((0, 0), (0, -1))), ((0, 0), ((-1, 0), (-1, -1))))
OUTER = (
    ((0, 0), ((1, 1), (1, 0))),
    ((0, 0), ((0, 1), (-1, 1))),
    ((0, 0), ((1, -1),)),
)
RING = (
    ((1, 0), ((0, 0), (0, -1))),
    ((0, 1), ((0, 0), (-1, 0))),
    ((1, 1), ((0, 0),)),
)
OUTSIDE = ((1, 1), (1, 0), (1, -1), (0, 1), (-1, 1))


def near(p, q):
    return abs(p[0] - q[0]) <= 1 and abs(p[1] - q[1]) <= 1


def offset(dr, dc):
    return (dr + 1) * 3 + dc + 1


class Corner:
    def __init__(self, n):
        self.a, self.b = 1 + n // 2, 1 + lax.rem(n, 2)
        self.down, self.across = 2 * self.a - 3, 2 * self.b - 3

    def at(self, src, dst):
        i = self.a + src[0] * self.down
        j = self.b + src[1] * self.across
        return i, j, offset((dst[0] - src[0]) * self.down, (dst[1] - src[1]) * self.across)

    def index(self, src, dst):
        i, j, k = self.at(src, dst)
        return i * 4 + j, k

    def get(self, ref, src, dst):
        return ref[self.index(src, dst)]

    def keep(self, pat, src, dst):
        if max(src) == 1:
            src, dst = dst, src
        i, j, k = self.at(src, dst)
        return pat[i - 1, j - 1, k].astype(jnp.float32)


def sends(symmetric):
    plan = {}
    for side in SIDES:
        if side[0] == 0:
            c = 2 if side[1] == 1 else 1
            first = [((1, c), (1, c)), ((2, c), (2, c)), ((1, c), (2, c))]
            later = [((1, c), (0, c)), ((2, c), (3, c))]
            relay = []
        else:
            r = 2 if side[0] == 1 else 1
            o = r + side[0]
            first = [((r, 1), (r, 1)), ((r, 2), (r, 2)), ((r, 1), (r, 2))]
            later = [((r, 1), (r, 0)), ((r, 2), (r, 3)), ((r, 1), (o, 0)), ((r, 2), (o, 3))]
            relay = [((r, 0), (r, 0)), ((r, 3), (r, 3))]
        if not symmetric:
            first = first + [(q, p) for p, q in first if p != q]
            later = later + [(q, p) for p, q in later]
        plan[side] = (first, later, relay)
    return plan


def kernel(rows, cols, pat, start, out, x0, s0, x1, s1, send_sem, recv_sem):
    row, col = lax.axis_index("row"), lax.axis_index("col")
    block = start.shape[-1]

    def device(side):
        return (lax.rem(row + side[0] + rows, rows), lax.rem(col + side[1] + cols, cols))

    barrier = pltpu.get_barrier_semaphore()
    for side in SIDES:
        pl.semaphore_signal(barrier, inc=1, device_id=device(side), device_id_type=MESH)

    def copies(phase, group, sides=SIDES):
        table = tables[phase]
        result = []
        for d, side in enumerate(SIDES):
            if side not in sides:
                continue
            groups = sends(phase < 2)[side]
            base = sum(len(g) for g in groups[:group])
            for n, (p, q) in enumerate(groups[group]):
                k = offset(q[0] - p[0], q[1] - p[1])
                here = p[0] * 4 + p[1]
                there = here - 2 * (side[0] * 4 + side[1])
                result.append(
                    pltpu.make_async_remote_copy(
                        src_ref=table.at[here, k],
                        dst_ref=table.at[there, k],
                        send_sem=send_sem.at[phase, d, base + n],
                        recv_sem=recv_sem.at[phase, d, base + n],
                        device_id=device(side),
                        device_id_type=MESH,
                    )
                )
        return result

    tables = (x0, s0, x1, s1)

    def begin(phase, group):
        for c in copies(phase, group):
            c.start()

    def arrive(phase, group, sides=SIDES):
        for c in copies(phase, group, sides):
            c.wait_recv()

    def pass_on(phase):
        arrive(phase, 0, SIDES[:2])
        begin(phase, 2)

    def settle(phase):
        arrive(phase, 0, SIDES[2:])
        arrive(phase, 1)
        arrive(phase, 2)

    def corners(body):
        def step(n, carry):
            body(Corner(n))
            return carry

        lax.fori_loop(0, 4, step, 0)

    def product(left, right, groups, emit):
        zero = jnp.zeros((block, block), jnp.float32)

        def body(c):
            for src, dsts in groups:
                mids = [
                    (i, j)
                    for i in (-1, 0, 1)
                    for j in (-1, 0, 1)
                    if near(src, (i, j)) and any(near((i, j), d) for d in dsts)
                ]
                lhs = jnp.concatenate([c.get(left, src, m) for m in mids], axis=1)
                rhs = jnp.concatenate(
                    [
                        jnp.concatenate([c.get(right, m, d) if near(m, d) else zero for d in dsts], axis=1)
                        for m in mids
                    ],
                    axis=0,
                )
                total = jnp.dot(lhs, rhs, precision=lax.Precision.HIGH, preferred_element_type=jnp.float32)
                for n, d in enumerate(dsts):
                    value = total[:, n * block : (n + 1) * block]
                    emit(c, src, d, c.keep(pat, src, d) * value)

        corners(body)

    def mirror(table):
        def body(c):
            for src, dst in (((0, 1), (1, 1)), ((1, 0), (1, 1)), ((1, 0), (0, 1))):
                table[c.index(dst, src)] = c.get(table, src, dst).T

        corners(body)
        for p, q in (((0, 1), (0, 2)), ((3, 1), (3, 2)), ((1, 0), (2, 0)), ((1, 3), (2, 3))):
            k = offset(q[0] - p[0], q[1] - p[1])
            table[q[0] * 4 + q[1], 8 - k] = table[p[0] * 4 + p[1], k].T

    def mask(c):
        for i in (-1, 0, 1):
            for j in (-1, 0, 1):
                here = (0, 0)
                a, b, k = c.at(here, (i, j))
                value = c.keep(pat, here, (i, j)) * start[a - 1, b - 1, k]
                x0[c.index(here, (i, j))] = value
                if max(i, j) == 1:
                    x0[c.index((i, j), here)] = value.T

    def square(c, src, dst, value):
        s0[c.index(src, dst)] = value
        if max(dst) == 1:
            s0[c.index(dst, src)] = value.T

    def advance(c, src, dst, value):
        x1[c.index(src, dst)] = 1.5 * c.get(x0, src, dst) - 0.5 * value

    def square_again(c, src, dst, value):
        s1[c.index(src, dst)] = value

    def finish(c, src, dst, value):
        a, b, k = c.at(src, dst)
        out[a - 1, b - 1, k] = 1.5 * c.get(x1, src, dst) - 0.5 * value

    corners(mask)
    pl.semaphore_wait(barrier, len(SIDES))
    begin(0, 0)
    begin(0, 1)
    product(x0, x0, INNER, square)
    begin(1, 0)
    pass_on(0)
    settle(0)
    mirror(x0)
    product(x0, x0, OUTER, square)
    begin(1, 1)
    product(x0, s0, INNER, advance)
    begin(2, 0)
    pass_on(1)
    product(x0, s0, RING, advance)
    settle(1)
    mirror(s0)
    product(x0, s0, OUTER, advance)
    begin(2, 1)
    product(x1, x1, INNER, square_again)
    begin(3, 0)
    pass_on(2)
    settle(2)
    product(x1, x1, OUTER, square_again)
    product(x1, x1, RING, square_again)
    begin(3, 1)
    product(x1, s1, INNER, finish)
    pass_on(3)
    settle(3)
    product(x1, s1, OUTER, finish)
    for phase in range(4):
        for group in range(3):
            for c in copies(phase, group):
                c.wait_send()


def solution(mesh):
    rows, cols = mesh.shape["row"], mesh.shape["col"]

    def step(pattern, start):
        block = start.shape[-1]
        return pl.pallas_call(
            functools.partial(kernel, rows, cols),
            out_shape=jax.ShapeDtypeStruct(start.shape, jnp.float32),
            in_specs=[pl.BlockSpec(memory_space=pltpu.SMEM), pl.BlockSpec(memory_space=pltpu.VMEM)],
            out_specs=pl.BlockSpec(memory_space=pltpu.VMEM),
            scratch_shapes=[pltpu.VMEM((16, 9, block, block), jnp.float32)] * 4
            + [pltpu.SemaphoreType.DMA((4, 4, 14))] * 2,
            compiler_params=pltpu.CompilerParams(
                collective_id=0, has_side_effects=True, vmem_limit_bytes=56 * 1024 * 1024
            ),
            cost_estimate=pl.CostEstimate(
                flops=2 * 976 * block**3, bytes_accessed=2 * start.size * 4, transcendentals=0
            ),
        )(pattern, start)

    return jax.shard_map(
        step,
        mesh=mesh,
        in_specs=(P("row", "col", None), P("row", "col", None, None, None)),
        out_specs=P("row", "col", None, None, None),
        check_vma=False,
    )
```

```python
import functools

import jax
import jax.numpy as jnp
from jax import lax
from jax.experimental import pallas as pl
from jax.experimental.pallas import tpu as pltpu
from jax.sharding import PartitionSpec as P

MESH = pl.DeviceIdType.MESH
INNER = (((0, 0), ((0, 0), (0, -1))), ((0, 0), ((-1, 0), (-1, -1))))
OUTER = (
    ((0, 0), ((1, 1), (1, 0))),
    ((0, 0), ((0, 1), (-1, 1))),
    ((0, 0), ((1, -1),)),
)
RING = (
    ((1, 0), ((0, 0), (0, -1))),
    ((0, 1), ((0, 0), (-1, 0))),
    ((1, 1), ((0, 0),)),
)
FLIPS = (((0, 1), (1, 1)), ((1, 0), (1, 1)), ((1, 0), (0, 1)))
OUTSIDE = ((1, 1), (1, 0), (1, -1), (0, 1), (-1, 1))
KINDS = {
    "x_self": (1, (0, 0), (0, 0), 0),
    "x_side": (1, (0, 0), (-1, 0), 2),
    "x_pair": (1, (0, 0), (1, 0), 4),
    "x_back": (1, (1, 0), (0, 0), 6),
    "y_self": (0, (0, 0), (0, 0), 0),
    "y_side": (0, (0, 0), (0, -1), 2),
    "y_pair": (0, (0, 0), (0, 1), 4),
    "y_diag": (0, (0, 0), (1, 1), 6),
    "y_back": (0, (0, 1), (0, 0), 8),
    "y_gaid": (0, (1, 1), (0, 0), 10),
    "relay": (0, (0, 1), (0, 1), 12),
}
FIRST = ("x_self", "y_self", "x_side", "y_side")
PAIRS = ("x_pair", "y_pair", "y_diag")
BACKS = ("x_back", "y_back", "y_gaid")


def near(p, q):
    return abs(p[0] - q[0]) <= 1 and abs(p[1] - q[1]) <= 1


class Corner:
    def __init__(self, n):
        self.n = n
        self.a, self.b = 1 + n // 2, 1 + lax.rem(n, 2)
        self.down, self.across = 2 * self.a - 3, 2 * self.b - 3

    def at(self, src, dst):
        i = self.a + src[0] * self.down
        j = self.b + src[1] * self.across
        k = 4 + 3 * (dst[0] - src[0]) * self.down + (dst[1] - src[1]) * self.across
        return i, j, k

    def index(self, src, dst):
        i, j, k = self.at(src, dst)
        return i * 4 + j, k

    def get(self, ref, src, dst):
        return ref[self.index(src, dst)]

    def keep(self, pat, src, dst):
        if max(src) == 1:
            src, dst = dst, src
        i, j, k = self.at(src, dst)
        return pat[i - 1, j - 1, k].astype(jnp.float32)


def kernel(rows, cols, pat, start, out, tile, x0, s0, x1, s1, send_sem, recv_sem, load_sem, store_sem):
    row, col = lax.axis_index("row"), lax.axis_index("col")
    block = start.shape[-1]
    tables = (x0, s0, x1, s1)

    def device(side):
        return (lax.rem(row + side[0] + rows, rows), lax.rem(col + side[1] + cols, cols))

    def load(c):
        return pltpu.make_async_copy(start.at[c.a - 1, c.b - 1], tile.at[c.n], load_sem.at[c.n])

    def store(c):
        return pltpu.make_async_copy(tile.at[c.n], out.at[c.a - 1, c.b - 1], store_sem.at[c.n])

    def corners(body):
        def step(n, carry):
            body(Corner(n))
            return carry

        lax.fori_loop(0, 4, step, 0)

    def guarded(phase, kind, c, action):
        if phase < 2 and kind in ("x_side", "y_side"):
            pl.when((c.a if kind == "x_side" else c.b) == 1)(action)
        else:
            action()

    def outgoing(phase, kind, c):
        axis, src, dst, slot = KINDS[kind]
        site, k = c.index(src, dst)
        if axis == 1:
            there, to, d, slot = site - 2 * c.across, device((0, c.across)), 2 - c.b, slot + c.a - 1
        else:
            there, to, d, slot = site - 8 * c.down, device((c.down, 0)), 4 - c.a, slot + c.b - 1
        return pltpu.make_async_remote_copy(
            src_ref=tables[phase].at[site, k],
            dst_ref=tables[phase].at[there, k],
            send_sem=send_sem.at[phase, d, slot],
            recv_sem=recv_sem.at[phase, d, slot],
            device_id=to,
            device_id_type=MESH,
        )

    def incoming(phase, kind, c):
        axis, src, dst, slot = KINDS[kind]
        if axis == 1:
            src, dst = (src[0], 1 - src[1]), (dst[0], 1 - dst[1])
            d, slot = c.b - 1, slot + c.a - 1
        else:
            src, dst = (1 - src[0], src[1]), (1 - dst[0], dst[1])
            d, slot = c.a + 1, slot + c.b - 1
        landing = tables[phase].at[c.index(src, dst)]
        return pltpu.make_async_remote_copy(
            src_ref=landing,
            dst_ref=landing,
            send_sem=send_sem.at[phase, d, slot],
            recv_sem=recv_sem.at[phase, d, slot],
            device_id=device((0, c.across) if axis == 1 else (c.down, 0)),
            device_id_type=MESH,
        )

    def send(phase, kinds, c):
        for kind in kinds:
            guarded(phase, kind, c, lambda kind=kind: outgoing(phase, kind, c).start())

    def receive(phase, kinds, c):
        for kind in kinds:
            guarded(phase, kind, c, lambda kind=kind: incoming(phase, kind, c).wait_recv())

    def pass_on(phase):
        def body(c):
            receive(phase, ("x_self",), c)
            send(phase, ("relay",), c)

        corners(body)

    def settle(phase):
        corners(lambda c: receive(phase, FIRST[1:] + (() if phase < 2 else BACKS), c))

    def product(c, left, right, groups, emit, flips=()):
        zero = jnp.zeros((block, block), jnp.float32)
        flipped = {}
        for src, dst in flips:
            flipped[dst, src] = c.get(right, src, dst).T
            right[c.index(dst, src)] = flipped[dst, src]

        def piece(m, d):
            if not near(m, d):
                return zero
            return flipped[m, d] if (m, d) in flipped else c.get(right, m, d)

        for src, dsts in groups:
            mids = [
                (i, j)
                for i in (-1, 0, 1)
                for j in (-1, 0, 1)
                if near(src, (i, j)) and any(near((i, j), d) for d in dsts)
            ]
            lhs = jnp.concatenate([c.get(left, src, m) for m in mids], axis=1)
            rhs = jnp.concatenate([jnp.concatenate([piece(m, d) for d in dsts], axis=1) for m in mids], axis=0)
            total = jnp.dot(lhs, rhs, precision=lax.Precision.HIGH, preferred_element_type=jnp.float32)
            for n, d in enumerate(dsts):
                emit(c, src, d, c.keep(pat, src, d) * total[:, n * block : (n + 1) * block])

    def mirror(table):
        for p, q in (((0, 1), (0, 2)), ((3, 1), (3, 2)), ((1, 0), (2, 0)), ((1, 3), (2, 3))):
            k = 4 + 3 * (q[0] - p[0]) + q[1] - p[1]
            table[q[0] * 4 + q[1], 8 - k] = table[p[0] * 4 + p[1], k].T

    def fold(table):
        def body(c):
            for dst in OUTSIDE:
                table[c.index(dst, (0, 0))] = c.get(table, (0, 0), dst).T

        corners(body)

    def square(c, src, dst, value):
        s0[c.index(src, dst)] = value

    def advance(c, src, dst, value):
        x1[c.index(src, dst)] = 1.5 * c.get(x0, src, dst) - 0.5 * value

    def square_again(c, src, dst, value):
        s1[c.index(src, dst)] = value

    def finish(c, src, dst, value):
        tile[c.n, c.at(src, dst)[2]] = 1.5 * c.get(x1, src, dst) - 0.5 * value

    def mask(c):
        load(c).wait()
        for k in range(9):
            x0[c.a * 4 + c.b, k] = pat[c.a - 1, c.b - 1, k].astype(jnp.float32) * tile[c.n, k]
        send(0, FIRST + PAIRS, c)

    def square_inside(c):
        product(c, x0, x0, INNER, square)
        send(1, FIRST, c)

    def square_outside(c):
        receive(0, PAIRS + ("relay",), c)
        product(c, x0, x0, OUTER, square, FLIPS)
        send(1, PAIRS, c)

    def advance_inside(c):
        product(c, x0, s0, INNER, advance)
        send(2, FIRST, c)

    def advance_ring(c):
        product(c, x0, s0, RING, advance)
        send(2, BACKS, c)

    def advance_outside(c):
        receive(1, PAIRS + ("relay",), c)
        product(c, x0, s0, OUTER, advance, FLIPS)
        send(2, PAIRS, c)

    def square_again_inside(c):
        product(c, x1, x1, INNER, square_again)
        send(3, FIRST, c)

    def square_again_outside(c):
        receive(2, PAIRS + ("relay",), c)
        product(c, x1, x1, OUTER, square_again)
        send(3, PAIRS, c)
        product(c, x1, x1, RING, square_again)
        send(3, BACKS, c)

    def finish_outside(c):
        receive(3, PAIRS + ("relay",), c)
        product(c, x1, s1, OUTER, finish)
        store(c).start()

    corners(lambda c: load(c).start())
    barrier = pltpu.get_barrier_semaphore()
    sides = ((0, 1), (0, -1), (1, 0), (-1, 0))
    for side in sides:
        pl.semaphore_signal(barrier, inc=1, device_id=device(side), device_id_type=MESH)
    pl.semaphore_wait(barrier, len(sides))
    corners(mask)
    fold(x0)
    corners(square_inside)
    pass_on(0)
    settle(0)
    mirror(x0)
    corners(square_outside)
    pass_on(1)
    fold(s0)
    corners(advance_inside)
    corners(advance_ring)
    settle(1)
    mirror(s0)
    corners(advance_outside)
    pass_on(2)
    corners(square_again_inside)
    settle(2)
    corners(square_again_outside)
    pass_on(3)
    corners(lambda c: product(c, x1, s1, INNER, finish))
    settle(3)
    corners(finish_outside)

    def drain(c):
        store(c).wait()
        for phase in range(4):
            for kind in KINDS:
                if phase >= 2 or kind not in BACKS:
                    guarded(phase, kind, c, lambda p=phase, k=kind: outgoing(p, k, c).wait_send())

    corners(drain)


def solution(mesh):
    rows, cols = mesh.shape["row"], mesh.shape["col"]

    def step(pattern, start):
        block = start.shape[-1]
        return pl.pallas_call(
            functools.partial(kernel, rows, cols),
            out_shape=jax.ShapeDtypeStruct(start.shape, jnp.float32),
            in_specs=[pl.BlockSpec(memory_space=pltpu.SMEM), pl.BlockSpec(memory_space=pl.ANY)],
            out_specs=pl.BlockSpec(memory_space=pl.ANY),
            scratch_shapes=[pltpu.VMEM((4, 9, block, block), jnp.float32)]
            + [pltpu.VMEM((16, 9, block, block), jnp.float32)] * 4
            + [pltpu.SemaphoreType.DMA((4, 4, 14))] * 2
            + [pltpu.SemaphoreType.DMA((4,))] * 2,
            compiler_params=pltpu.CompilerParams(
                collective_id=0, has_side_effects=True, vmem_limit_bytes=56 * 1024 * 1024
            ),
            cost_estimate=pl.CostEstimate(
                flops=2 * 976 * block**3, bytes_accessed=2 * start.size * 4, transcendentals=0
            ),
        )(pattern, start)

    return jax.shard_map(
        step,
        mesh=mesh,
        in_specs=(P("row", "col", None), P("row", "col", None, None, None)),
        out_specs=P("row", "col", None, None, None),
        check_vma=False,
    )
```

```python
import functools

import jax
import jax.numpy as jnp
from jax import lax
from jax.experimental import pallas as pl
from jax.experimental.pallas import tpu as pltpu
from jax.sharding import PartitionSpec as P

MESH = pl.DeviceIdType.MESH
INNER = (((0, 0), ((0, 0), (0, -1))), ((0, 0), ((-1, 0), (-1, -1))))
OUTER = (
    ((0, 0), ((1, 1), (1, 0))),
    ((0, 0), ((0, 1), (-1, 1))),
    ((0, 0), ((1, -1),)),
)
RING = (
    ((1, 0), ((0, 0), (0, -1))),
    ((0, 1), ((0, 0), (-1, 0))),
    ((1, 1), ((0, 0),)),
)
FLIPS = (((0, 1), (1, 1)), ((1, 0), (1, 1)), ((1, 0), (0, 1)))
OUTSIDE = ((1, 1), (1, 0), (1, -1), (0, 1), (-1, 1))
KINDS = {
    "x_self": (1, (0, 0), (0, 0), 0),
    "x_side": (1, (0, 0), (-1, 0), 2),
    "x_pair": (1, (0, 0), (1, 0), 4),
    "x_back": (1, (1, 0), (0, 0), 6),
    "y_self": (0, (0, 0), (0, 0), 0),
    "y_side": (0, (0, 0), (0, -1), 2),
    "y_pair": (0, (0, 0), (0, 1), 4),
    "y_diag": (0, (0, 0), (1, 1), 6),
    "y_back": (0, (0, 1), (0, 0), 8),
    "y_gaid": (0, (1, 1), (0, 0), 10),
    "relay": (0, (0, 1), (0, 1), 12),
    "hop": (0, (0, 1), (1, 1), 14),
}
FIRST = ("x_self", "y_self", "x_side", "y_side")
PAIRS = ("x_pair", "y_pair", "y_diag")
BACKS = ("x_back", "y_back", "y_gaid")


def near(p, q):
    return abs(p[0] - q[0]) <= 1 and abs(p[1] - q[1]) <= 1


class Corner:
    def __init__(self, step, core):
        self.step = step
        half = step // 2
        self.inner = half == 1
        self.a, self.b = 1 + half + core * (1 - 2 * half), 1 + lax.rem(step, 2)
        self.n = 2 * self.a + self.b - 3
        self.down, self.across = 2 * self.a - 3, 2 * self.b - 3

    def at(self, src, dst):
        i = self.a + src[0] * self.down
        j = self.b + src[1] * self.across
        k = 4 + 3 * (dst[0] - src[0]) * self.down + (dst[1] - src[1]) * self.across
        return i, j, k

    def index(self, src, dst):
        i, j, k = self.at(src, dst)
        return i * 4 + j, k

    def get(self, ref, src, dst):
        return ref[self.index(src, dst)]

    def keep(self, pat, src, dst):
        if max(src) == 1:
            src, dst = dst, src
        i, j, k = self.at(src, dst)
        return pat[i - 1, j - 1, k].astype(jnp.float32)


def kernel(rows, cols, pat, start, out, tile, x0, s0, x1, s1, send_sem, recv_sem, load_sem):
    row, col = lax.axis_index("row"), lax.axis_index("col")
    block = start.shape[-1]
    tables = (x0, s0, x1, s1)

    def device(side):
        return (lax.rem(row + side[0] + rows, rows), lax.rem(col + side[1] + cols, cols))

    def load(c):
        return pltpu.make_async_copy(start.at[c.a - 1, c.b - 1], tile.at[c.n], load_sem.at[c.n])

    def corners(body):
        def step(n, carry):
            body(Corner(n, lax.rem(row, 2)))
            return carry

        lax.fori_loop(0, 4, step, 0)

    def guarded(phase, kind, c, action):
        if phase < 2 and kind in ("x_side", "y_side"):
            pl.when((c.a if kind == "x_side" else c.b) == 1)(action)
        elif kind == "x_back":
            pl.when(jnp.logical_not(c.inner))(action)
        elif kind == "hop":
            pl.when(c.inner)(action)
        else:
            action()

    def outgoing(phase, kind, c):
        axis, src, dst, slot = KINDS[kind]
        site, k = c.index(src, dst)
        if axis == 1:
            there, to, d, slot = site - 2 * c.across, device((0, c.across)), 2 - c.b, slot + c.a - 1
        else:
            there, to, d, slot = site - 8 * c.down, device((c.down, 0)), 4 - c.a, slot + c.b - 1
        return pltpu.make_async_remote_copy(
            src_ref=tables[phase].at[site, k],
            dst_ref=tables[phase].at[there, k],
            send_sem=send_sem.at[phase, d, slot],
            recv_sem=recv_sem.at[phase, d, slot],
            device_id=to,
            device_id_type=MESH,
        )

    def incoming(phase, kind, c):
        axis, src, dst, slot = KINDS[kind]
        if axis == 1:
            src, dst = (src[0], 1 - src[1]), (dst[0], 1 - dst[1])
            d, slot = c.b - 1, slot + c.a - 1
        else:
            src, dst = (1 - src[0], src[1]), (1 - dst[0], dst[1])
            d, slot = c.a + 1, slot + c.b - 1
        landing = tables[phase].at[c.index(src, dst)]
        return pltpu.make_async_remote_copy(
            src_ref=landing,
            dst_ref=landing,
            send_sem=send_sem.at[phase, d, slot],
            recv_sem=recv_sem.at[phase, d, slot],
            device_id=device((0, c.across) if axis == 1 else (c.down, 0)),
            device_id_type=MESH,
        )

    def send(phase, kinds, c):
        for kind in kinds:
            guarded(phase, kind, c, lambda kind=kind: outgoing(phase, kind, c).start())

    def receive(phase, kinds, c):
        for kind in kinds:
            guarded(phase, kind, c, lambda kind=kind: incoming(phase, kind, c).wait_recv())

    def pass_on(phase):
        def body(c):
            receive(phase, ("x_self",), c)
            send(phase, ("relay",), c)

        corners(body)

    def collect(phase, c):
        @pl.when(c.step == 1)
        def _():
            for step in (2, 3):
                other = Corner(step, lax.rem(row, 2))
                receive(phase, ("x_pair",), other)
                send(phase, ("hop",), other)

        pl.when(jnp.logical_not(c.inner))(lambda: receive(phase, ("x_pair",), c))
        receive(phase, PAIRS[1:] + ("hop", "relay"), c)

    def settle(phase):
        corners(lambda c: receive(phase, FIRST[1:] + (() if phase < 2 else BACKS), c))

    def product(c, left, right, groups, emit, flips=()):
        zero = jnp.zeros((block, block), jnp.float32)
        flipped = {}
        for src, dst in flips:
            flipped[dst, src] = c.get(right, src, dst).T
            right[c.index(dst, src)] = flipped[dst, src]

        def piece(m, d):
            if not near(m, d):
                return zero
            return flipped[m, d] if (m, d) in flipped else c.get(right, m, d)

        for src, dsts in groups:
            mids = [
                (i, j)
                for i in (-1, 0, 1)
                for j in (-1, 0, 1)
                if near(src, (i, j)) and any(near((i, j), d) for d in dsts)
            ]
            lhs = jnp.concatenate([c.get(left, src, m) for m in mids], axis=1)
            rhs = jnp.concatenate([jnp.concatenate([piece(m, d) for d in dsts], axis=1) for m in mids], axis=0)
            total = jnp.dot(lhs, rhs, precision=lax.Precision.HIGH, preferred_element_type=jnp.float32)
            for n, d in enumerate(dsts):
                emit(c, src, d, c.keep(pat, src, d) * total[:, n * block : (n + 1) * block])

    def mirror(table):
        for p, q in (((0, 1), (0, 2)), ((3, 1), (3, 2)), ((1, 0), (2, 0)), ((1, 3), (2, 3))):
            k = 4 + 3 * (q[0] - p[0]) + q[1] - p[1]
            table[q[0] * 4 + q[1], 8 - k] = table[p[0] * 4 + p[1], k].T

    def fold(c):
        for dst in OUTSIDE:
            x0[c.index(dst, (0, 0))] = c.get(x0, (0, 0), dst).T

    def square(c, src, dst, value):
        s0[c.index(src, dst)] = value
        if max(dst) == 1:
            s0[c.index(dst, src)] = value.T

    def advance(c, src, dst, value):
        x1[c.index(src, dst)] = 1.5 * c.get(x0, src, dst) - 0.5 * value

    def square_again(c, src, dst, value):
        s1[c.index(src, dst)] = value

    def finish(c, src, dst, value):
        out[c.a - 1, c.b - 1, c.at(src, dst)[2]] = 1.5 * c.get(x1, src, dst) - 0.5 * value

    def mask(c):
        load(c).wait()
        for k in range(9):
            x0[c.a * 4 + c.b, k] = pat[c.a - 1, c.b - 1, k].astype(jnp.float32) * tile[c.n, k]
        send(0, FIRST + PAIRS, c)

    def square_inside(c):
        product(c, x0, x0, INNER, square)
        send(1, FIRST, c)

    def square_outside(c):
        receive(0, PAIRS + ("relay",), c)
        product(c, x0, x0, OUTER, square, FLIPS)
        send(1, PAIRS, c)

    def advance_inside(c):
        product(c, x0, s0, INNER, advance)
        send(2, FIRST, c)

    def advance_ring(c):
        product(c, x0, s0, RING, advance)
        send(2, BACKS, c)

    def advance_outside(c):
        receive(1, PAIRS + ("relay",), c)
        product(c, x0, s0, OUTER, advance, FLIPS)
        send(2, PAIRS, c)

    def square_again_inside(c):
        product(c, x1, x1, INNER, square_again)
        send(3, FIRST, c)

    def square_again_outside(c):
        collect(2, c)
        product(c, x1, x1, OUTER, square_again)
        send(3, PAIRS, c)
        product(c, x1, x1, RING, square_again)
        send(3, BACKS, c)

    def finish_outside(c):
        collect(3, c)
        product(c, x1, s1, OUTER, finish)

    corners(lambda c: load(c).start())
    barrier = pltpu.get_barrier_semaphore()
    sides = ((0, 1), (0, -1), (1, 0), (-1, 0))
    for side in sides:
        pl.semaphore_signal(barrier, inc=1, device_id=device(side), device_id_type=MESH)
    pl.semaphore_wait(barrier, len(sides))
    corners(mask)
    corners(fold)
    corners(square_inside)
    pass_on(0)
    settle(0)
    mirror(x0)
    corners(square_outside)
    pass_on(1)
    corners(advance_inside)
    corners(advance_ring)
    settle(1)
    mirror(s0)
    corners(advance_outside)
    pass_on(2)
    corners(square_again_inside)
    settle(2)
    corners(square_again_outside)
    pass_on(3)
    corners(lambda c: product(c, x1, s1, INNER, finish))
    settle(3)
    corners(finish_outside)

    def drain(c):
        for phase in range(4):
            for kind in KINDS:
                if phase >= 2 or kind not in BACKS + ("hop",):
                    guarded(phase, kind, c, lambda p=phase, k=kind: outgoing(p, k, c).wait_send())

    corners(drain)


def solution(mesh):
    rows, cols = mesh.shape["row"], mesh.shape["col"]

    def step(pattern, start):
        block = start.shape[-1]
        return pl.pallas_call(
            functools.partial(kernel, rows, cols),
            out_shape=pltpu.VMEM(start.shape, jnp.float32),
            in_specs=[pl.BlockSpec(memory_space=pltpu.SMEM), pl.BlockSpec(memory_space=pl.ANY)],
            out_specs=pl.BlockSpec(memory_space=pltpu.VMEM),
            scratch_shapes=[pltpu.VMEM((4, 9, block, block), jnp.float32)]
            + [pltpu.VMEM((16, 9, block, block), jnp.float32)] * 4
            + [pltpu.SemaphoreType.DMA((4, 4, 16))] * 2
            + [pltpu.SemaphoreType.DMA((4,))],
            compiler_params=pltpu.CompilerParams(
                collective_id=0, has_side_effects=True, vmem_limit_bytes=60 * 1024 * 1024
            ),
            cost_estimate=pl.CostEstimate(
                flops=2 * 976 * block**3, bytes_accessed=2 * start.size * 4, transcendentals=0
            ),
        )(pattern, start)

    return jax.shard_map(
        step,
        mesh=mesh,
        in_specs=(P("row", "col", None), P("row", "col", None, None, None)),
        out_specs=P("row", "col", None, None, None),
        check_vma=False,
    )
```

```python
import functools

import jax
import jax.numpy as jnp
from jax import lax
from jax.experimental import pallas as pl
from jax.experimental.pallas import tpu as pltpu
from jax.sharding import PartitionSpec as P

MESH = pl.DeviceIdType.MESH
INNER = (((0, 0), ((0, 0), (0, -1))), ((0, 0), ((-1, 0), (-1, -1))))
OUTER = (
    ((0, 0), ((1, 1), (1, 0))),
    ((0, 0), ((0, 1), (-1, 1))),
    ((0, 0), ((1, -1),)),
)
RING = (
    ((1, 0), ((0, 0), (0, -1))),
    ((0, 1), ((0, 0), (-1, 0))),
    ((1, 1), ((0, 0),)),
)
FLIPS = (((0, 1), (1, 1)), ((1, 0), (1, 1)), ((1, 0), (0, 1)))
LATE = ((0, 1), (1, 0), (1, 1))
OUTSIDE = ((1, 1), (1, 0), (1, -1), (0, 1), (-1, 1))
KINDS = {
    "x_self": (1, (0, 0), (0, 0), 0),
    "x_side": (1, (0, 0), (-1, 0), 2),
    "x_pair": (1, (0, 0), (1, 0), 4),
    "x_back": (1, (1, 0), (0, 0), 6),
    "y_self": (0, (0, 0), (0, 0), 0),
    "y_side": (0, (0, 0), (0, -1), 2),
    "y_pair": (0, (0, 0), (0, 1), 4),
    "y_diag": (0, (0, 0), (1, 1), 6),
    "y_back": (0, (0, 1), (0, 0), 8),
    "y_gaid": (0, (1, 1), (0, 0), 10),
    "relay": (0, (0, 1), (0, 1), 12),
    "hop": (0, (0, 1), (1, 1), 14),
}
FIRST = ("x_self", "y_self", "x_side", "y_side")
PAIRS = ("x_pair", "y_pair", "y_diag")
BACKS = ("x_back", "y_back", "y_gaid")


def near(p, q):
    return abs(p[0] - q[0]) <= 1 and abs(p[1] - q[1]) <= 1


class Corner:
    def __init__(self, step, core):
        self.step = step
        half = step // 2
        self.inner = half == 1
        self.a, self.b = 1 + half + core * (1 - 2 * half), 1 + lax.rem(step, 2)
        self.n = 2 * self.a + self.b - 3
        self.down, self.across = 2 * self.a - 3, 2 * self.b - 3

    def at(self, src, dst):
        i = self.a + src[0] * self.down
        j = self.b + src[1] * self.across
        k = 4 + 3 * (dst[0] - src[0]) * self.down + (dst[1] - src[1]) * self.across
        return i, j, k

    def index(self, src, dst):
        i, j, k = self.at(src, dst)
        return i * 4 + j, k

    def get(self, ref, src, dst):
        return ref[self.index(src, dst)]

    def keep(self, pat, src, dst):
        if max(src) == 1:
            src, dst = dst, src
        i, j, k = self.at(src, dst)
        return pat[i - 1, j - 1, k].astype(jnp.float32)


def kernel(rows, cols, pat, start, out, tile, x0, s0, x1, s1, send_sem, recv_sem, load_sem):
    row, col = lax.axis_index("row"), lax.axis_index("col")
    block = start.shape[-1]
    tables = (x0, s0, x1, s1)

    def device(side):
        return (lax.rem(row + side[0] + rows, rows), lax.rem(col + side[1] + cols, cols))

    def load(c):
        return pltpu.make_async_copy(start.at[c.a - 1, c.b - 1], tile.at[c.n], load_sem.at[c.n])

    def corners(body):
        def step(n, carry):
            body(Corner(n, lax.rem(row, 2)))
            return carry

        lax.fori_loop(0, 4, step, 0)

    def guarded(phase, kind, c, action):
        if phase < 2 and kind in ("x_side", "y_side"):
            pl.when((c.a if kind == "x_side" else c.b) == 1)(action)
        elif kind == "x_back":
            pl.when(jnp.logical_not(c.inner))(action)
        elif kind == "hop":
            pl.when(c.inner)(action)
        else:
            action()

    def outgoing(phase, kind, c):
        axis, src, dst, slot = KINDS[kind]
        site, k = c.index(src, dst)
        if axis == 1:
            there, to, d, slot = site - 2 * c.across, device((0, c.across)), 2 - c.b, slot + c.a - 1
        else:
            there, to, d, slot = site - 8 * c.down, device((c.down, 0)), 4 - c.a, slot + c.b - 1
        return pltpu.make_async_remote_copy(
            src_ref=tables[phase].at[site, k],
            dst_ref=tables[phase].at[there, k],
            send_sem=send_sem.at[phase, d, slot],
            recv_sem=recv_sem.at[phase, d, slot],
            device_id=to,
            device_id_type=MESH,
        )

    def incoming(phase, kind, c):
        axis, src, dst, slot = KINDS[kind]
        if axis == 1:
            src, dst = (src[0], 1 - src[1]), (dst[0], 1 - dst[1])
            d, slot = c.b - 1, slot + c.a - 1
        else:
            src, dst = (1 - src[0], src[1]), (1 - dst[0], dst[1])
            d, slot = c.a + 1, slot + c.b - 1
        landing = tables[phase].at[c.index(src, dst)]
        return pltpu.make_async_remote_copy(
            src_ref=landing,
            dst_ref=landing,
            send_sem=send_sem.at[phase, d, slot],
            recv_sem=recv_sem.at[phase, d, slot],
            device_id=device((0, c.across) if axis == 1 else (c.down, 0)),
            device_id_type=MESH,
        )

    def send(phase, kinds, c):
        for kind in kinds:
            guarded(phase, kind, c, lambda kind=kind: outgoing(phase, kind, c).start())

    def receive(phase, kinds, c):
        for kind in kinds:
            guarded(phase, kind, c, lambda kind=kind: incoming(phase, kind, c).wait_recv())

    def pass_on(phase, steps=(0, 1, 2, 3)):
        for step in steps:
            c = Corner(step, lax.rem(row, 2))
            receive(phase, ("x_self",), c)
            send(phase, ("relay",), c)

    def collect(phase, c):
        @pl.when(c.step == 1)
        def _():
            for step in (2, 3):
                other = Corner(step, lax.rem(row, 2))
                receive(phase, ("x_pair",), other)
                send(phase, ("hop",), other)

        pl.when(jnp.logical_not(c.inner))(lambda: receive(phase, ("x_pair",), c))
        receive(phase, PAIRS[1:] + ("hop", "relay"), c)

    def settle(phase):
        corners(lambda c: receive(phase, FIRST[1:], c))

    def sent(phases, kinds):
        def body(c):
            for phase in phases:
                for kind in kinds:
                    guarded(phase, kind, c, lambda p=phase, k=kind: outgoing(p, k, c).wait_send())

        corners(body)

    def product(c, left, right, groups, emit, flips=(), leave=(), only=None):
        zero = jnp.zeros((block, block), jnp.float32)
        flipped = {}
        for src, dst in flips:
            flipped[dst, src] = c.get(right, src, dst).T
            right[c.index(dst, src)] = flipped[dst, src]

        def piece(m, d):
            if not near(m, d):
                return zero
            return flipped[m, d] if (m, d) in flipped else c.get(right, m, d)

        for src, dsts in groups:
            mids = [
                (i, j)
                for i in (-1, 0, 1)
                for j in (-1, 0, 1)
                if near(src, (i, j)) and any(near((i, j), d) for d in dsts)
                if (i, j) not in leave and (only is None or (i, j) in only)
            ]
            lhs = jnp.concatenate([c.get(left, src, m) for m in mids], axis=1)
            rhs = jnp.concatenate([jnp.concatenate([piece(m, d) for d in dsts], axis=1) for m in mids], axis=0)
            total = jnp.dot(lhs, rhs, precision=lax.Precision.HIGH, preferred_element_type=jnp.float32)
            for n, d in enumerate(dsts):
                emit(c, src, d, c.keep(pat, src, d) * total[:, n * block : (n + 1) * block])

    def mirror(table):
        for p, q in (((0, 1), (0, 2)), ((3, 1), (3, 2)), ((1, 0), (2, 0)), ((1, 3), (2, 3))):
            k = 4 + 3 * (q[0] - p[0]) + q[1] - p[1]
            table[q[0] * 4 + q[1], 8 - k] = table[p[0] * 4 + p[1], k].T

    def fold(c):
        for dst in OUTSIDE:
            x0[c.index(dst, (0, 0))] = c.get(x0, (0, 0), dst).T

    def square(c, src, dst, value):
        s0[c.index(src, dst)] = value
        if max(dst) == 1:
            s0[c.index(dst, src)] = value.T

    def advance(c, src, dst, value):
        x1[c.index(src, dst)] = 1.5 * c.get(x0, src, dst) - 0.5 * value

    def square_again(c, src, dst, value):
        s1[c.index(src, dst)] = value

    def finish(c, src, dst, value):
        out[c.a - 1, c.b - 1, c.at(src, dst)[2]] = 1.5 * c.get(x1, src, dst) - 0.5 * value

    def complete(c, src, dst, value):
        out[c.a - 1, c.b - 1, c.at(src, dst)[2]] -= 0.5 * value

    def mask(c):
        load(c).wait()
        for k in range(9):
            x0[c.a * 4 + c.b, k] = pat[c.a - 1, c.b - 1, k].astype(jnp.float32) * tile[c.n, k]
        send(0, FIRST + PAIRS, c)

    def square_inside(c):
        product(c, x0, x0, INNER, square)
        send(1, FIRST, c)

    def square_outside(c):
        receive(0, PAIRS + ("relay",), c)
        product(c, x0, x0, OUTER, square, FLIPS)
        send(1, PAIRS, c)

    def advance_inside(c):
        product(c, x0, s0, INNER, advance)
        send(2, FIRST, c)

    def advance_ring(c):
        product(c, x0, s0, RING, advance)
        send(2, BACKS, c)

    def advance_outside(c):
        pl.when(c.step == 2)(lambda: pass_on(2, (0, 1)))
        receive(1, PAIRS + ("relay",), c)
        product(c, x0, s0, OUTER, advance, FLIPS)
        send(2, PAIRS, c)

    def square_again_inside(c):
        product(c, x1, x1, INNER, square_again)
        send(3, FIRST, c)

    def square_again_outside(c):
        pl.when(c.step == 3)(lambda: pass_on(3, (0, 1)))
        receive(2, BACKS, c)
        collect(2, c)
        product(c, x1, x1, OUTER, square_again)
        send(3, PAIRS, c)
        product(c, x1, x1, RING, square_again)
        send(3, BACKS, c)

    def finish_early(c):
        product(c, x1, s1, OUTER[2:], finish)
        product(c, x1, s1, OUTER[:2], finish, leave=LATE)

    def finish_outside(c):
        receive(3, BACKS, c)
        collect(3, c)
        product(c, x1, s1, OUTER[:2], complete, only=LATE)

    corners(lambda c: load(c).start())
    barrier = pltpu.get_barrier_semaphore()
    sides = ((0, 1), (0, -1), (1, 0), (-1, 0))
    for side in sides:
        pl.semaphore_signal(barrier, inc=1, device_id=device(side), device_id_type=MESH)
    pl.semaphore_wait(barrier, len(sides))
    corners(mask)
    corners(fold)
    corners(square_inside)
    pass_on(0)
    settle(0)
    mirror(x0)
    corners(square_outside)
    pass_on(1)
    corners(advance_inside)
    corners(advance_ring)
    settle(1)
    mirror(s0)
    corners(advance_outside)
    pass_on(2, (2, 3))
    corners(square_again_inside)
    settle(2)
    corners(square_again_outside)
    pass_on(3, (2, 3))
    corners(lambda c: product(c, x1, s1, INNER, finish))
    sent((0, 1), FIRST + PAIRS + ("relay",))
    sent((2,), FIRST + BACKS + PAIRS + ("hop", "relay"))
    settle(3)
    corners(finish_early)
    sent((3,), FIRST + BACKS)
    corners(finish_outside)
    sent((3,), PAIRS + ("hop", "relay"))


def solution(mesh):
    rows, cols = mesh.shape["row"], mesh.shape["col"]

    def step(pattern, start):
        block = start.shape[-1]
        return pl.pallas_call(
            functools.partial(kernel, rows, cols),
            out_shape=pltpu.VMEM(start.shape, jnp.float32),
            in_specs=[pl.BlockSpec(memory_space=pltpu.SMEM), pl.BlockSpec(memory_space=pl.ANY)],
            out_specs=pl.BlockSpec(memory_space=pltpu.VMEM),
            scratch_shapes=[pltpu.VMEM((4, 9, block, block), jnp.float32)]
            + [pltpu.VMEM((16, 9, block, block), jnp.float32)] * 4
            + [pltpu.SemaphoreType.DMA((4, 4, 16))] * 2
            + [pltpu.SemaphoreType.DMA((4,))],
            compiler_params=pltpu.CompilerParams(
                collective_id=0, has_side_effects=True, vmem_limit_bytes=60 * 1024 * 1024
            ),
            cost_estimate=pl.CostEstimate(
                flops=2 * 976 * block**3, bytes_accessed=2 * start.size * 4, transcendentals=0
            ),
        )(pattern, start)

    return jax.shard_map(
        step,
        mesh=mesh,
        in_specs=(P("row", "col", None), P("row", "col", None, None, None)),
        out_specs=P("row", "col", None, None, None),
        check_vma=False,
    )
```

```python
import functools

import jax
import jax.numpy as jnp
from jax import lax
from jax.experimental import pallas as pl
from jax.experimental.pallas import tpu as pltpu
from jax.sharding import PartitionSpec as P

MESH = pl.DeviceIdType.MESH
INNER = (((0, 0), ((0, 0), (0, -1))), ((0, 0), ((-1, 0), (-1, -1))))
OUTER = (
    ((0, 0), ((1, 1), (1, 0))),
    ((0, 0), ((0, 1), (-1, 1))),
    ((0, 0), ((1, -1),)),
)
RING = (
    ((1, 0), ((0, 0), (0, -1))),
    ((0, 1), ((0, 0), (-1, 0))),
    ((1, 1), ((0, 0),)),
)
FLIPS = (((0, 1), (1, 1)), ((1, 0), (1, 1)), ((1, 0), (0, 1)))
LATE = ((0, 1), (1, 0), (1, 1))
OUTSIDE = ((1, 1), (1, 0), (1, -1), (0, 1), (-1, 1))
KINDS = {
    "x_self": (1, (0, 0), (0, 0), 0),
    "x_side": (1, (0, 0), (-1, 0), 2),
    "x_pair": (1, (0, 0), (1, 0), 4),
    "x_back": (1, (1, 0), (0, 0), 6),
    "y_self": (0, (0, 0), (0, 0), 0),
    "y_side": (0, (0, 0), (0, -1), 2),
    "y_pair": (0, (0, 0), (0, 1), 4),
    "y_diag": (0, (0, 0), (1, 1), 6),
    "y_back": (0, (0, 1), (0, 0), 8),
    "y_gaid": (0, (1, 1), (0, 0), 10),
    "relay": (0, (0, 1), (0, 1), 12),
    "hop": (0, (0, 1), (1, 1), 14),
}
FIRST = ("x_self", "y_self", "x_side", "y_side")
PAIRS = ("x_pair", "y_pair", "y_diag")
BACKS = ("x_back", "y_back", "y_gaid")


def near(p, q):
    return abs(p[0] - q[0]) <= 1 and abs(p[1] - q[1]) <= 1


class Corner:
    def __init__(self, step, core):
        self.step = step
        half = step // 2
        self.inner = half == 1
        self.a, self.b = 1 + half + core * (1 - 2 * half), 1 + lax.rem(step, 2)
        self.n = 2 * self.a + self.b - 3
        self.down, self.across = 2 * self.a - 3, 2 * self.b - 3

    def at(self, src, dst):
        i = self.a + src[0] * self.down
        j = self.b + src[1] * self.across
        k = 4 + 3 * (dst[0] - src[0]) * self.down + (dst[1] - src[1]) * self.across
        return i, j, k

    def index(self, src, dst):
        i, j, k = self.at(src, dst)
        return i * 4 + j, k

    def get(self, ref, src, dst):
        return ref[self.index(src, dst)]

    def keep(self, pat, src, dst):
        if max(src) == 1:
            src, dst = dst, src
        i, j, k = self.at(src, dst)
        return pat[i - 1, j - 1, k].astype(jnp.float32)


def kernel(rows, cols, pat, start, out, tile, x0, s0, x1, s1, send_sem, recv_sem, load_sem):
    row, col = lax.axis_index("row"), lax.axis_index("col")
    block = start.shape[-1]
    tables = (x0, s0, x1, s1)

    def device(side):
        return (lax.rem(row + side[0] + rows, rows), lax.rem(col + side[1] + cols, cols))

    def load(c):
        return pltpu.make_async_copy(start.at[c.a - 1, c.b - 1], tile.at[c.n], load_sem.at[c.n])

    def corners(body):
        def step(n, carry):
            body(Corner(n, lax.rem(row, 2)))
            return carry

        lax.fori_loop(0, 4, step, 0)

    def guarded(phase, kind, c, action):
        if phase < 2 and kind in ("x_side", "y_side"):
            pl.when((c.a if kind == "x_side" else c.b) == 1)(action)
        elif kind == "x_back":
            pl.when(jnp.logical_not(c.inner))(action)
        elif kind == "hop":
            pl.when(c.inner)(action)
        else:
            action()

    def outgoing(phase, kind, c):
        axis, src, dst, slot = KINDS[kind]
        site, k = c.index(src, dst)
        if axis == 1:
            there, to, d, slot = site - 2 * c.across, device((0, c.across)), 2 - c.b, slot + c.a - 1
        else:
            there, to, d, slot = site - 8 * c.down, device((c.down, 0)), 4 - c.a, slot + c.b - 1
        return pltpu.make_async_remote_copy(
            src_ref=tables[phase].at[site, k],
            dst_ref=tables[phase].at[there, k],
            send_sem=send_sem.at[phase, d, slot],
            recv_sem=recv_sem.at[phase, d, slot],
            device_id=to,
            device_id_type=MESH,
        )

    def incoming(phase, kind, c):
        axis, src, dst, slot = KINDS[kind]
        if axis == 1:
            src, dst = (src[0], 1 - src[1]), (dst[0], 1 - dst[1])
            d, slot = c.b - 1, slot + c.a - 1
        else:
            src, dst = (1 - src[0], src[1]), (1 - dst[0], dst[1])
            d, slot = c.a + 1, slot + c.b - 1
        landing = tables[phase].at[c.index(src, dst)]
        return pltpu.make_async_remote_copy(
            src_ref=landing,
            dst_ref=landing,
            send_sem=send_sem.at[phase, d, slot],
            recv_sem=recv_sem.at[phase, d, slot],
            device_id=device((0, c.across) if axis == 1 else (c.down, 0)),
            device_id_type=MESH,
        )

    def send(phase, kinds, c):
        for kind in kinds:
            guarded(phase, kind, c, lambda kind=kind: outgoing(phase, kind, c).start())

    def receive(phase, kinds, c):
        for kind in kinds:
            guarded(phase, kind, c, lambda kind=kind: incoming(phase, kind, c).wait_recv())

    def pass_on(phase, steps=(0, 1, 2, 3)):
        for step in steps:
            c = Corner(step, lax.rem(row, 2))
            receive(phase, ("x_self",), c)
            send(phase, ("relay",), c)

    def collect(phase, c):
        @pl.when(c.step == 1)
        def _():
            for step in (2, 3):
                other = Corner(step, lax.rem(row, 2))
                receive(phase, ("x_pair",), other)
                send(phase, ("hop",), other)

        pl.when(jnp.logical_not(c.inner))(lambda: receive(phase, ("x_pair",), c))
        receive(phase, PAIRS[1:] + ("hop", "relay"), c)

    def settle(phase):
        corners(lambda c: receive(phase, FIRST[1:], c))

    def sent(phases, kinds):
        def body(c):
            for phase in phases:
                for kind in kinds:
                    guarded(phase, kind, c, lambda p=phase, k=kind: outgoing(p, k, c).wait_send())

        corners(body)

    def product(c, left, right, groups, emit, flips=(), leave=(), only=None):
        zero = jnp.zeros((block, block), jnp.float32)
        flipped = {}
        for src, dst in flips:
            flipped[dst, src] = c.get(right, src, dst).T
            right[c.index(dst, src)] = flipped[dst, src]

        def piece(m, d):
            if not near(m, d):
                return zero
            return flipped[m, d] if (m, d) in flipped else c.get(right, m, d)

        for src, dsts in groups:
            mids = [
                (i, j)
                for i in (-1, 0, 1)
                for j in (-1, 0, 1)
                if near(src, (i, j)) and any(near((i, j), d) for d in dsts)
                if (i, j) not in leave and (only is None or (i, j) in only)
            ]
            lhs = jnp.concatenate([c.get(left, src, m) for m in mids], axis=1)
            rhs = jnp.concatenate([jnp.concatenate([piece(m, d) for d in dsts], axis=1) for m in mids], axis=0)
            total = jnp.dot(lhs, rhs, precision=lax.Precision.HIGH, preferred_element_type=jnp.float32)
            for n, d in enumerate(dsts):
                emit(c, src, d, c.keep(pat, src, d) * total[:, n * block : (n + 1) * block])

    def mirror(table):
        for p, q in (((0, 1), (0, 2)), ((3, 1), (3, 2)), ((1, 0), (2, 0)), ((1, 3), (2, 3))):
            k = 4 + 3 * (q[0] - p[0]) + q[1] - p[1]
            table[q[0] * 4 + q[1], 8 - k] = table[p[0] * 4 + p[1], k].T

    def fold(c):
        for dst in OUTSIDE:
            x0[c.index(dst, (0, 0))] = c.get(x0, (0, 0), dst).T

    def square(c, src, dst, value):
        s0[c.index(src, dst)] = value
        if max(dst) == 1:
            s0[c.index(dst, src)] = value.T

    def advance(c, src, dst, value):
        x1[c.index(src, dst)] = 1.5 * c.get(x0, src, dst) - 0.5 * value

    def square_again(c, src, dst, value):
        s1[c.index(src, dst)] = value

    def finish(c, src, dst, value):
        out[c.a - 1, c.b - 1, c.at(src, dst)[2]] = 1.5 * c.get(x1, src, dst) - 0.5 * value

    def complete(c, src, dst, value):
        out[c.a - 1, c.b - 1, c.at(src, dst)[2]] -= 0.5 * value

    def mask(c):
        load(c).wait()
        for k in range(9):
            x0[c.a * 4 + c.b, k] = pat[c.a - 1, c.b - 1, k].astype(jnp.float32) * tile[c.n, k]
        send(0, FIRST + PAIRS, c)

    def square_inside(c):
        product(c, x0, x0, INNER, square)
        send(1, FIRST, c)

    def square_outside(c):
        receive(0, PAIRS + ("relay",), c)
        product(c, x0, x0, OUTER, square, FLIPS)
        send(1, PAIRS, c)

    def advance_inside(c):
        product(c, x0, s0, INNER, advance)
        send(2, FIRST, c)

    def advance_ring(c):
        product(c, x0, s0, RING, advance)
        send(2, BACKS, c)

    def advance_outside(c):
        pl.when(c.step == 2)(lambda: pass_on(2, (0, 1)))
        receive(1, PAIRS + ("relay",), c)
        product(c, x0, s0, OUTER, advance, FLIPS)
        send(2, PAIRS, c)

    def square_again_inside(c):
        product(c, x1, x1, INNER, square_again)
        send(3, FIRST, c)

    def square_again_outside(c):
        pl.when(c.step == 3)(lambda: pass_on(3, (0, 1)))
        receive(2, BACKS, c)
        collect(2, c)
        product(c, x1, x1, OUTER[:1], square_again)
        send(3, ("x_pair", "y_diag"), c)
        product(c, x1, x1, OUTER[1:2], square_again)
        send(3, ("y_pair",), c)
        product(c, x1, x1, RING, square_again)
        send(3, BACKS, c)

    def finish_early(c):
        product(c, x1, s1, OUTER[2:], finish)
        product(c, x1, s1, OUTER[:2], finish, leave=LATE)

    def finish_outside(c):
        receive(3, BACKS, c)
        collect(3, c)
        product(c, x1, s1, OUTER[:2], complete, only=LATE)

    corners(lambda c: load(c).start())
    barrier = pltpu.get_barrier_semaphore()
    sides = ((0, 1), (0, -1), (1, 0), (-1, 0))
    for side in sides:
        pl.semaphore_signal(barrier, inc=1, device_id=device(side), device_id_type=MESH)
    pl.semaphore_wait(barrier, len(sides))
    corners(mask)
    corners(fold)
    corners(square_inside)
    pass_on(0)
    settle(0)
    mirror(x0)
    corners(square_outside)
    pass_on(1)
    corners(advance_inside)
    corners(advance_ring)
    settle(1)
    mirror(s0)
    corners(advance_outside)
    pass_on(2, (2, 3))
    corners(square_again_inside)
    settle(2)
    corners(square_again_outside)
    pass_on(3, (2, 3))
    corners(lambda c: product(c, x1, x1, OUTER[2:], square_again))
    corners(lambda c: product(c, x1, s1, INNER, finish))
    sent((0, 1), FIRST + PAIRS + ("relay",))
    sent((2,), FIRST + BACKS + PAIRS + ("hop", "relay"))
    settle(3)
    corners(finish_early)
    sent((3,), FIRST + BACKS)
    corners(finish_outside)
    sent((3,), PAIRS + ("hop", "relay"))


def solution(mesh):
    rows, cols = mesh.shape["row"], mesh.shape["col"]

    def step(pattern, start):
        block = start.shape[-1]
        return pl.pallas_call(
            functools.partial(kernel, rows, cols),
            out_shape=pltpu.VMEM(start.shape, jnp.float32),
            in_specs=[pl.BlockSpec(memory_space=pltpu.SMEM), pl.BlockSpec(memory_space=pl.ANY)],
            out_specs=pl.BlockSpec(memory_space=pltpu.VMEM),
            scratch_shapes=[pltpu.VMEM((4, 9, block, block), jnp.float32)]
            + [pltpu.VMEM((16, 9, block, block), jnp.float32)] * 4
            + [pltpu.SemaphoreType.DMA((4, 4, 16))] * 2
            + [pltpu.SemaphoreType.DMA((4,))],
            compiler_params=pltpu.CompilerParams(
                collective_id=0, has_side_effects=True, vmem_limit_bytes=60 * 1024 * 1024
            ),
            cost_estimate=pl.CostEstimate(
                flops=2 * 976 * block**3, bytes_accessed=2 * start.size * 4, transcendentals=0
            ),
        )(pattern, start)

    return jax.shard_map(
        step,
        mesh=mesh,
        in_specs=(P("row", "col", None), P("row", "col", None, None, None)),
        out_specs=P("row", "col", None, None, None),
        check_vma=False,
    )
```
